32 devices in a mesh: dp: 8 (over y, x, core), slab: 4 (over z).
Axes of the slice: x: 2, y: 2, z: 4, core: 2. Of those that a mesh axis runs over, the one named last changes fastest.
Arguments:
- images: bfloat16 [8, 256, 32, 128], P('dp', 'slab'), may hold values from -6 to 6
- cotangent: bfloat16 [8, 128, 64, 256], P('dp', None, 'slab'), may hold values from -6 to 6
- kernel: bfloat16 [3, 3, 256, 128], replicated, may hold values from -0.125 to 0.125
Outputs:
- grad_images: bfloat16 [8, 256, 32, 128], P('dp', 'slab')
- grad_kernel: float32 [3, 3, 256, 128], replicated
The draws below stay inside these ranges and needn't reach their ends.
All inputs are finite; a program needn't handle non-finite values.
Results may differ from the reference program's by a relative error of at most 0.0034.
Values may be sent and summed in bfloat16 or wider, within the bound.
A program may use at most 64 MiB of HBM per device.

```python
import jax
import jax.numpy as jnp
from jax import lax

CIN = 256
COUT = 128
H_LO = 32
W_LO = 128
IMAGES = 8
H_UP = 64
W_UP = 256


def block_scale(rng, extent, cuts, low, largest):
    factor_of = 1.0
    for position, shards_of in cuts:
        heights = jax.random.uniform(jax.random.fold_in(jax.random.fold_in(rng, 6), position), (shards_of,), jnp.float32, low / len(cuts), largest / len(cuts))
        factor_of = factor_of * jnp.repeat(jnp.exp(heights), extent[position] // shards_of).reshape((-1,) + (1,) * (len(extent) - 1 - position))
    return factor_of


def centred(stream_key, shape, width, bound, split=(), dtype=jnp.bfloat16):
    factor_of = block_scale(stream_key, shape, split, -0.22, 0.18) if split else 1.0
    result = jax.random.normal(stream_key, shape, jnp.float32) * width * factor_of
    return jnp.minimum(jnp.maximum(result, -bound), bound).astype(dtype)


def setup_inputs(seed: int = 0) -> dict:
    keys = jax.random.split(jax.random.key(seed), 4)
    return {
        "images": centred(keys[0], (IMAGES, CIN, H_LO, W_LO), 1.0, 6.0, ((0, 8), (1, 4))),
        "cotangent": centred(keys[1], (IMAGES, COUT, H_UP, W_UP), 1.0, 6.0, ((0, 8), (2, 4))),
        "kernel": centred(keys[2], (3, 3, CIN, COUT), (9 * CIN) ** -0.5, 0.125),
    }


def upsample(field):
    return jnp.repeat(jnp.repeat(field, 2, axis=2), 2, axis=3)


def downsum(field):
    count, chans, rows, cols = field.shape
    return field.reshape(count, chans, rows // 2, 2, cols // 2, 2).sum(axis=(3, 5))


def kernel_terms(padded_up, grad_rows):
    return lax.conv_general_dilated(padded_up, grad_rows, (1, 1), ((0, 0), (1, 1)), dimension_numbers=("CNHW", "IOHW", "HWNC"), preferred_element_type=jnp.float32)


def input_terms(padded_grad, kernel):
    flipped = kernel[::-1, ::-1]
    return lax.conv_general_dilated(padded_grad, flipped, (1, 1), ((0, 0), (1, 1)), dimension_numbers=("NCHW", "HWOI", "NCHW"), preferred_element_type=jnp.float32)


def reference(images, cotangent, kernel):
    batch_img = images.reshape(IMAGES, 1, CIN, H_LO, W_LO)
    batch_grad = cotangent.reshape(IMAGES, 1, COUT, H_UP, W_UP)

    def step(total, pair):
        block_img, block_grad = pair
        upsampled = upsample(block_img)
        padded_up = jnp.pad(upsampled, ((0, 0), (0, 0), (1, 1), (0, 0)))
        padded_grad = jnp.pad(block_grad, ((0, 0), (0, 0), (1, 1), (0, 0)))
        total = total + kernel_terms(padded_up, block_grad)
        grad_low = downsum(input_terms(padded_grad, kernel)).astype(jnp.bfloat16)
        return total, grad_low

    start = jnp.zeros((3, 3, CIN, COUT), jnp.float32)
    grad_kernel, grad_low = lax.scan(step, start, (batch_img, batch_grad))
    return grad_low.reshape(IMAGES, CIN, H_LO, W_LO), grad_kernel
```

```python
import functools

import jax
import jax.numpy as jnp
from jax import lax
from jax.experimental import pallas as pl
from jax.experimental.pallas import tpu as pltpu
from jax.sharding import PartitionSpec as P

MESH = pl.DeviceIdType.MESH
BF16 = jnp.bfloat16
F32 = jnp.float32


def each(low, high, step):
    if high - low <= 8:
        for index in range(low, high):
            step(index)
    else:
        lax.fori_loop(low, high, lambda index, carry: (step(index), carry)[1], 0)


def kernel(
    images, cotangent, weights, grad_images, grad_kernel,
    wide, rows_up, box, pairs, flat, image_send, image_all, image_wide, input_send, input_all, input_wide,
    term_send, term_all, term_sum, total,
    halo_out, halo_in, image_out, image_in, input_out, input_in, term_out, term_in, sum_out, sum_in,
    slab_out, slab_in, dp_out, dp_in,
):
    slabs, parts = lax.axis_size("slab"), lax.axis_size("dp")
    me, part = lax.axis_index("slab"), lax.axis_index("dp")
    chans, low_rows, low_cols = images.shape
    outs, rows, cols = cotangent.shape
    all_chans = chans * slabs
    taps = weights.shape[0]
    own_rows = rows // 2
    shard = term_all.shape[2]

    def slab_at(distance):
        return lax.rem(me + distance + slabs, slabs)

    def part_at(distance):
        return lax.rem(part + distance + parts, parts)

    barrier = pltpu.get_barrier_semaphore()
    each(1, slabs, lambda r: pl.semaphore_signal(barrier, inc=1, device_id={"slab": slab_at(r)}, device_id_type=MESH))
    each(1, parts, lambda j: pl.semaphore_signal(barrier, inc=1, device_id={"dp": part_at(j)}, device_id_type=MESH))

    def remote(src, dst, send, recv, device):
        return pltpu.make_async_remote_copy(
            src_ref=src, dst_ref=dst, send_sem=send, recv_sem=recv, device_id=device, device_id_type=MESH
        )

    for o in range(0, outs, 16):
        for half in range(cols // 128):
            part_of = cotangent[pl.ds(o, 16), :, pl.ds(half * 128, 128)]
            wide[half, pl.ds(o * rows, 16 * rows), :] = part_of.astype(F32).reshape(16 * rows, 128)

    def turn(row):
        for half in range(cols // 128):
            rows_up[:, pl.ds((row + 1) * cols + half * 128, 128)] = wide[
                half, pl.ds(row, outs, stride=rows), :
            ].astype(BF16)

    turn(0)
    turn(rows - 1)
    pl.semaphore_wait(barrier, slabs - 1 + parts - 1)

    first, last = pl.ds(0, cols), pl.ds((rows + 1) * cols, cols)
    head = remote(rows_up.at[:, pl.ds(cols, cols)], rows_up.at[:, last], halo_out.at[0], halo_in.at[0], {"slab": slab_at(-1)})
    tail = remote(rows_up.at[:, pl.ds(rows * cols, cols)], rows_up.at[:, first], halo_out.at[1], halo_in.at[1], {"slab": slab_at(1)})

    @pl.when(me > 0)
    def _():
        head.start()

    @pl.when(me < slabs - 1)
    def _():
        tail.start()

    image_wide[...] = images[...].astype(F32).reshape(chans * low_rows, low_cols)

    def image_block(dst, slab):
        for p in range(own_rows):
            dst[:, pl.ds(p * low_cols, low_cols)] = image_wide[
                pl.ds(slab * own_rows + p, chans, stride=low_rows), :
            ].astype(BF16)

    image_copies = [None]
    for r in range(1, slabs):
        target = slab_at(-r)
        image_block(image_send.at[r], target)
        copy = remote(image_send.at[r], image_all.at[r], image_out.at[r], image_in.at[r], {"slab": target})
        copy.start()
        image_copies.append(copy)
    image_block(image_all.at[0], me)

    for row in range(1, rows - 1):
        turn(row)

    j = lax.broadcasted_iota(jnp.int32, (cols, low_cols), 0)
    q = lax.broadcasted_iota(jnp.int32, (cols, low_cols), 1)
    for b in range(3):
        gap = j - 2 * q + b
        hit = jnp.where((gap == 1) | (gap == 2), 1.0, 0.0).astype(BF16)
        pairs[pl.ds(0, cols), pl.ds(b * low_cols, low_cols)] = hit
        pairs[pl.ds(cols, cols), pl.ds(b * low_cols, low_cols)] = hit
    for tap in range(taps):
        flat[:, pl.ds(tap * outs, outs)] = weights[tap]

    def box_row(p, a):
        start = (2 * p - a + 2) * cols
        if not isinstance(p, int):
            start = pl.multiple_of(start, 128)
        sums = jnp.dot(rows_up[:, pl.ds(start, 2 * cols)], pairs[...], preferred_element_type=F32).astype(BF16)
        at = p * low_cols
        if not isinstance(p, int):
            at = pl.multiple_of(at, 128)
        for b in range(3):
            box[pl.ds((a * 3 + b) * outs, outs), pl.ds(at, low_cols)] = sums[:, b * low_cols:(b + 1) * low_cols]

    def inner(p, carry):
        for a in range(3):
            box_row(p, a)
        return carry

    lax.fori_loop(1, own_rows - 1, inner, 0)
    box_row(0, 0)
    box_row(0, 1)
    box_row(own_rows - 1, 1)
    box_row(own_rows - 1, 2)

    @pl.when(me > 0)
    def _():
        tail.wait_recv()

    @pl.when(me == 0)
    def _():
        rows_up[:, first] = jnp.zeros((outs, cols), BF16)

    @pl.when(me < slabs - 1)
    def _():
        head.wait_recv()

    @pl.when(me == slabs - 1)
    def _():
        rows_up[:, last] = jnp.zeros((outs, cols), BF16)

    box_row(0, 2)
    box_row(own_rows - 1, 0)

    used = taps * chans
    padded = parts * shard

    def terms(r):
        product = lax.dot_general(
            image_all[r], box[...], (((1,), (1,)), ((), ())), preferred_element_type=F32
        ).astype(BF16)
        for tap in range(taps):
            term_send[r, pl.ds(tap * chans, chans), :] = product[:, tap * outs:(tap + 1) * outs]
        if padded > used:
            term_send[r, pl.ds(used, padded - used), :] = jnp.zeros((padded - used, outs), BF16)

    def term_copy(r, step):
        peer = part_at(step)
        return remote(
            term_send.at[r, pl.ds(pl.multiple_of(peer * shard, 16), shard)], term_all.at[r, step],
            term_out.at[r, step], term_in.at[r, step], {"dp": peer},
        )

    sum_copies = [None] * slabs

    def gather_terms(r):
        acc = term_send[r, pl.ds(pl.multiple_of(part * shard, 16), shard), :].astype(F32)
        each(1, parts, lambda step: term_copy(r, step).wait_recv())
        if parts <= 8:
            for step in range(1, parts):
                acc = acc + term_all[r, step].astype(F32)
        else:
            acc = lax.fori_loop(1, parts, lambda step, value: value + term_all[r, step].astype(F32), acc)
        if r == 0:
            term_sum[0, 0] = acc
        else:
            term_sum[1, r] = acc
            copy = remote(term_sum.at[1, r], term_sum.at[0, r], sum_out.at[r], sum_in.at[r], {"slab": slab_at(r)})
            copy.start()
            sum_copies[r] = copy

    terms(0)
    each(1, parts, lambda step: term_copy(0, step).start())

    tile = 2 * low_cols
    for n in range(own_rows * low_cols // tile):
        at = pl.ds(n * tile, tile)
        input_send[:, at] = jnp.dot(flat[...], box[:, at], preferred_element_type=F32).astype(BF16)

    input_copies = [None]
    for r in range(1, slabs):
        image_copies[r].wait_recv()
        terms(r)
        each(1, parts, lambda step: term_copy(r, step).start())
        image_copies[r].wait_send()
        target = slab_at(-r)
        copy = remote(
            input_send.at[pl.ds(pl.multiple_of(target * chans, 16), chans)], input_all.at[me],
            input_out.at[r], input_in.at[r], {"slab": target},
        )
        copy.start()
        input_copies.append(copy)
        gather_terms(r - 1)
    gather_terms(slabs - 1)
    input_all[me] = input_send[pl.ds(pl.multiple_of(me * chans, 16), chans), :]

    for r in range(1, slabs):
        sum_copies[r].wait_recv()
    mine = pl.ds(pl.multiple_of(part * shard, 16), shard)
    total[me, mine, :] = functools.reduce(lambda x, y: x + y, [term_sum[0, r] for r in range(slabs)]).astype(BF16)

    slab_copies = [None]
    for r in range(1, slabs):
        copy = remote(total.at[me, mine], total.at[me, mine], slab_out.at[r], slab_in.at[r], {"slab": slab_at(r)})
        copy.start()
        slab_copies.append(copy)

    def dp_copy(r, step):
        source = slab_at(-r)
        return remote(total.at[source, mine], total.at[source, mine], dp_out.at[r, step], dp_in.at[r, step], {"dp": part_at(step)})

    each(1, parts, lambda step: dp_copy(0, step).start())
    for r in range(1, slabs):
        slab_copies[r].wait_recv()
        each(1, parts, lambda step: dp_copy(r, step).start())

    for r in range(1, slabs):
        input_copies[r].wait_recv()
    for s in range(slabs):
        for p in range(own_rows):
            input_wide[pl.ds(s * own_rows + p, chans, stride=low_rows), :] = input_all[
                s, :, pl.ds(p * low_cols, low_cols)
            ].astype(F32)
    grad_images[...] = input_wide[...].astype(BF16).reshape(chans, low_rows, low_cols)

    for r in range(slabs):
        each(1, parts, lambda step: dp_copy(r, step).wait_recv())
    for s in range(slabs):
        for tap in range(taps):
            grad_kernel[tap, pl.ds(s * chans, chans), :] = total[s, pl.ds(tap * chans, chans), :].astype(F32)

    @pl.when(me > 0)
    def _():
        head.wait_send()

    @pl.when(me < slabs - 1)
    def _():
        tail.wait_send()

    for r in range(1, slabs):
        input_copies[r].wait_send()
        sum_copies[r].wait_send()
        slab_copies[r].wait_send()
    for r in range(slabs):
        each(1, parts, lambda step: term_copy(r, step).wait_send())
        each(1, parts, lambda step: dp_copy(r, step).wait_send())


def body(images, cotangent, weights):
    slabs, parts = lax.axis_size("slab"), lax.axis_size("dp")
    _, chans, low_rows, low_cols = images.shape
    _, outs, rows, cols = cotangent.shape
    height, width, all_chans, _ = weights.shape
    taps = height * width
    own_rows = rows // 2
    area = own_rows * low_cols
    shard = -(-(taps * chans) // (parts * 16)) * 16
    dma = pltpu.SemaphoreType.DMA
    vmem = pl.BlockSpec(memory_space=pltpu.VMEM)
    grad_images, grad_kernel = pl.pallas_call(
        kernel,
        out_shape=(
            jax.ShapeDtypeStruct((chans, low_rows, low_cols), BF16),
            jax.ShapeDtypeStruct((taps, all_chans, outs), F32),
        ),
        in_specs=[vmem] * 3,
        out_specs=(vmem, vmem),
        scratch_shapes=[
            pltpu.VMEM((cols // 128, outs * rows, 128), F32),
            pltpu.VMEM((outs, (rows + 2) * cols), BF16),
            pltpu.VMEM((taps * outs, area), BF16),
            pltpu.VMEM((2 * cols, 3 * low_cols), BF16),
            pltpu.VMEM((all_chans, taps * outs), BF16),
            pltpu.VMEM((slabs, chans, area), BF16),
            pltpu.VMEM((slabs, chans, area), BF16),
            pltpu.VMEM((chans * low_rows, low_cols), F32),
            pltpu.VMEM((all_chans, area), BF16),
            pltpu.VMEM((slabs, chans, area), BF16),
            pltpu.VMEM((chans * low_rows, low_cols), F32),
            pltpu.VMEM((slabs, parts * shard, outs), BF16),
            pltpu.VMEM((slabs, parts, shard, outs), BF16),
            pltpu.VMEM((2, slabs, shard, outs), F32),
            pltpu.VMEM((slabs, parts * shard, outs), BF16),
            dma((2,)), dma((2,)), dma((slabs,)), dma((slabs,)), dma((slabs,)), dma((slabs,)),
            dma((slabs, parts)), dma((slabs, parts)), dma((slabs,)), dma((slabs,)),
            dma((slabs,)), dma((slabs,)), dma((slabs, parts)), dma((slabs, parts)),
        ],
        compiler_params=pltpu.CompilerParams(
            collective_id=0, has_side_effects=True, vmem_limit_bytes=48 * 1024 * 1024
        ),
    )(images[0], cotangent[0], weights.reshape(taps, all_chans, outs))
    return grad_images[None], grad_kernel.reshape(weights.shape)


def solution(mesh):
    placed = (P("dp", "slab", None, None), P("dp", None, "slab", None), P())
    return jax.shard_map(
        body,
        mesh=mesh,
        in_specs=placed,
        out_specs=(P("dp", "slab", None, None), P()),
        check_vma=False,
    )
```

```python
import functools

import jax
import jax.numpy as jnp
from jax import lax
from jax.experimental import pallas as pl
from jax.experimental.pallas import tpu as pltpu
from jax.sharding import PartitionSpec as P

MESH = pl.DeviceIdType.MESH
BF16 = jnp.bfloat16
F32 = jnp.float32


def each(low, high, step):
    if high - low <= 8:
        for index in range(low, high):
            step(index)
    else:
        lax.fori_loop(low, high, lambda index, carry: (step(index), carry)[1], 0)


def kernel(
    images_from, cotangent_from, weights_from, grad_images, grad_kernel,
    images, cotangent, weights, loads, wide, rows_up, box, pairs, flat, image_send, image_all, image_wide, input_send, input_all, input_wide,
    term_send, term_all, term_sum, total,
    halo_out, halo_in, image_out, image_in, input_out, input_in, term_out, term_in, sum_out, sum_in,
    slab_out, slab_in, dp_out, dp_in, core_out, core_in,
):
    slabs, parts = lax.axis_size("slab"), lax.axis_size("dp")
    me, part = lax.axis_index("slab"), lax.axis_index("dp")
    chans, low_rows, low_cols = images.shape
    outs, rows, cols = cotangent.shape
    all_chans = chans * slabs
    taps = weights.shape[0]
    own_rows = rows // 2
    shard = term_all.shape[2]
    cores = core_out.shape[2]
    chips = parts // cores
    core = lax.rem(part, cores)

    def slab_at(distance):
        return lax.rem(me + distance + slabs, slabs)

    def part_at(distance):
        return lax.rem(part + distance + parts, parts)

    load_images = pltpu.make_async_copy(images_from, images, loads.at[0])
    load_cotangent = pltpu.make_async_copy(cotangent_from, cotangent, loads.at[1])
    load_weights = pltpu.make_async_copy(weights_from, weights, loads.at[2])
    load_images.start()
    load_cotangent.start()
    load_weights.start()

    barrier = pltpu.get_barrier_semaphore()
    each(1, slabs, lambda r: pl.semaphore_signal(barrier, inc=1, device_id={"slab": slab_at(r)}, device_id_type=MESH))
    each(1, parts, lambda j: pl.semaphore_signal(barrier, inc=1, device_id={"dp": part_at(j)}, device_id_type=MESH))

    def remote(src, dst, send, recv, device):
        return pltpu.make_async_remote_copy(
            src_ref=src, dst_ref=dst, send_sem=send, recv_sem=recv, device_id=device, device_id_type=MESH
        )

    load_images.wait()
    image_wide[...] = images[...].astype(F32).reshape(chans * low_rows, low_cols)

    def image_block(dst, slab):
        for p in range(own_rows):
            dst[:, pl.ds(p * low_cols, low_cols)] = image_wide[
                pl.ds(slab * own_rows + p, chans, stride=low_rows), :
            ].astype(BF16)

    image_copies = [None]
    for r in range(1, slabs):
        target = slab_at(-r)
        image_block(image_send.at[r], target)
        if r == 1:
            pl.semaphore_wait(barrier, slabs - 1 + parts - 1)
        copy = remote(image_send.at[r], image_all.at[r], image_out.at[r], image_in.at[r], {"slab": target})
        copy.start()
        image_copies.append(copy)

    load_cotangent.wait()
    for o in range(0, outs, 16):
        for half in range(cols // 128):
            part_of = cotangent[pl.ds(o, 16), :, pl.ds(half * 128, 128)]
            wide[half, pl.ds(o * rows, 16 * rows), :] = part_of.astype(F32).reshape(16 * rows, 128)

    def turn(row):
        for half in range(cols // 128):
            rows_up[:, pl.ds((row + 1) * cols + half * 128, 128)] = wide[
                half, pl.ds(row, outs, stride=rows), :
            ].astype(BF16)

    turn(0)
    turn(rows - 1)

    first, last = pl.ds(0, cols), pl.ds((rows + 1) * cols, cols)
    head = remote(rows_up.at[:, pl.ds(cols, cols)], rows_up.at[:, last], halo_out.at[0], halo_in.at[0], {"slab": slab_at(-1)})
    tail = remote(rows_up.at[:, pl.ds(rows * cols, cols)], rows_up.at[:, first], halo_out.at[1], halo_in.at[1], {"slab": slab_at(1)})

    @pl.when(me > 0)
    def _():
        head.start()

    @pl.when(me < slabs - 1)
    def _():
        tail.start()

    image_block(image_all.at[0], me)

    for row in range(1, rows - 1):
        turn(row)

    j = lax.broadcasted_iota(jnp.int32, (cols, low_cols), 0)
    q = lax.broadcasted_iota(jnp.int32, (cols, low_cols), 1)
    for b in range(3):
        gap = j - 2 * q + b
        hit = jnp.where((gap == 1) | (gap == 2), 1.0, 0.0).astype(BF16)
        pairs[pl.ds(0, cols), pl.ds(b * low_cols, low_cols)] = hit
        pairs[pl.ds(cols, cols), pl.ds(b * low_cols, low_cols)] = hit
    load_weights.wait()
    for tap in range(taps):
        flat[:, pl.ds(tap * outs, outs)] = weights[tap]

    def box_row(p, a):
        start = (2 * p - a + 2) * cols
        if not isinstance(p, int):
            start = pl.multiple_of(start, 128)
        sums = jnp.dot(rows_up[:, pl.ds(start, 2 * cols)], pairs[...], preferred_element_type=F32).astype(BF16)
        at = p * low_cols
        if not isinstance(p, int):
            at = pl.multiple_of(at, 128)
        for b in range(3):
            box[pl.ds((a * 3 + b) * outs, outs), pl.ds(at, low_cols)] = sums[:, b * low_cols:(b + 1) * low_cols]

    def inner(p, carry):
        for a in range(3):
            box_row(p, a)
        return carry

    lax.fori_loop(1, own_rows - 1, inner, 0)
    box_row(0, 0)
    box_row(0, 1)
    box_row(own_rows - 1, 1)
    box_row(own_rows - 1, 2)

    @pl.when(me > 0)
    def _():
        tail.wait_recv()

    @pl.when(me == 0)
    def _():
        rows_up[:, first] = jnp.zeros((outs, cols), BF16)

    @pl.when(me < slabs - 1)
    def _():
        head.wait_recv()

    @pl.when(me == slabs - 1)
    def _():
        rows_up[:, last] = jnp.zeros((outs, cols), BF16)

    box_row(0, 2)
    box_row(own_rows - 1, 0)

    used = taps * chans
    padded = parts * shard

    def terms(r):
        product = lax.dot_general(
            image_all[r], box[...], (((1,), (1,)), ((), ())), preferred_element_type=F32
        ).astype(BF16)
        for tap in range(taps):
            term_send[r, pl.ds(tap * chans, chans), :] = product[:, tap * outs:(tap + 1) * outs]
        if padded > used:
            term_send[r, pl.ds(used, padded - used), :] = jnp.zeros((padded - used, outs), BF16)

    def term_copy(r, step):
        peer = part_at(step)
        return remote(
            term_send.at[r, pl.ds(pl.multiple_of(peer * shard, 16), shard)], term_all.at[r, step],
            term_out.at[r, step], term_in.at[r, step], {"dp": peer},
        )

    sum_copies = [None] * slabs

    def gather_terms(r):
        acc = term_send[r, pl.ds(pl.multiple_of(part * shard, 16), shard), :].astype(F32)
        each(1, parts, lambda step: term_copy(r, step).wait_recv())
        if parts <= 8:
            for step in range(1, parts):
                acc = acc + term_all[r, step].astype(F32)
        else:
            acc = lax.fori_loop(1, parts, lambda step, value: value + term_all[r, step].astype(F32), acc)
        if r == 0:
            term_sum[0, 0] = acc
        else:
            term_sum[1, r] = acc
            copy = remote(term_sum.at[1, r], term_sum.at[0, r], sum_out.at[r], sum_in.at[r], {"slab": slab_at(r)})
            copy.start()
            sum_copies[r] = copy

    terms(0)
    each(1, parts, lambda step: term_copy(0, step).start())

    tile = 2 * low_cols
    for n in range(own_rows * low_cols // tile):
        at = pl.ds(n * tile, tile)
        input_send[:, at] = jnp.dot(flat[...], box[:, at], preferred_element_type=F32).astype(BF16)

    input_copies = [None]
    for r in range(1, slabs):
        image_copies[r].wait_send()
        target = slab_at(-r)
        copy = remote(
            input_send.at[pl.ds(pl.multiple_of(target * chans, 16), chans)], input_all.at[me],
            input_out.at[r], input_in.at[r], {"slab": target},
        )
        copy.start()
        input_copies.append(copy)
        image_copies[r].wait_recv()
        terms(r)
        each(1, parts, lambda step: term_copy(r, step).start())
        gather_terms(r - 1)
    gather_terms(slabs - 1)
    input_all[me] = input_send[pl.ds(pl.multiple_of(me * chans, 16), chans), :]

    for r in range(1, slabs):
        sum_copies[r].wait_recv()
    mine = pl.ds(pl.multiple_of(part * shard, 16), shard)
    total[me, mine, :] = functools.reduce(lambda x, y: x + y, [term_sum[0, r] for r in range(slabs)]).astype(BF16)

    slab_copies = [None]
    for r in range(1, slabs):
        copy = remote(total.at[me, mine], total.at[me, mine], slab_out.at[r], slab_in.at[r], {"slab": slab_at(r)})
        copy.start()
        slab_copies.append(copy)

    def dp_copy(r, step):
        source = slab_at(-r)
        return remote(total.at[source, mine], total.at[source, mine], dp_out.at[r, step], dp_in.at[r, step], {"dp": part_at(step * cores)})

    def core_copy(r, step, other):
        source = slab_at(-r)
        at = pl.ds(pl.multiple_of(part_at(-step * cores) * shard, 16), shard)
        device = part - core + lax.rem(core + other, cores)
        return remote(
            total.at[source, at], total.at[source, at], core_out.at[r, step, other], core_in.at[r, step, other], {"dp": device}
        )

    def for_cores(r, step, act):
        for other in range(1, cores):
            act(core_copy(r, step, other))

    for r in range(slabs):
        if r:
            slab_copies[r].wait_recv()
        each(1, chips, lambda step: dp_copy(r, step).start())
        for_cores(r, 0, lambda copy: copy.start())

    def forward(r, step):
        dp_copy(r, step).wait_recv()
        for_cores(r, step, lambda copy: copy.start())

    for r in range(slabs):
        each(1, chips, lambda step: forward(r, step))

    for r in range(1, slabs):
        input_copies[r].wait_recv()
    for s in range(slabs):
        for p in range(own_rows):
            input_wide[pl.ds(s * own_rows + p, chans, stride=low_rows), :] = input_all[
                s, :, pl.ds(p * low_cols, low_cols)
            ].astype(F32)
    grad_images[...] = input_wide[...].astype(BF16).reshape(chans, low_rows, low_cols)

    for r in range(slabs):
        each(0, chips, lambda step: for_cores(r, step, lambda copy: copy.wait_recv()))
    for s in range(slabs):
        for tap in range(taps):
            grad_kernel[tap, pl.ds(s * chans, chans), :] = total[s, pl.ds(tap * chans, chans), :].astype(F32)

    @pl.when(me > 0)
    def _():
        head.wait_send()

    @pl.when(me < slabs - 1)
    def _():
        tail.wait_send()

    for r in range(1, slabs):
        input_copies[r].wait_send()
        sum_copies[r].wait_send()
        slab_copies[r].wait_send()
    for r in range(slabs):
        each(1, parts, lambda step: term_copy(r, step).wait_send())
        each(1, chips, lambda step: dp_copy(r, step).wait_send())
        each(0, chips, lambda step: for_cores(r, step, lambda copy: copy.wait_send()))


def body(images, cotangent, weights):
    slabs, parts = lax.axis_size("slab"), lax.axis_size("dp")
    _, chans, low_rows, low_cols = images.shape
    _, outs, rows, cols = cotangent.shape
    height, width, all_chans, _ = weights.shape
    taps = height * width
    own_rows = rows // 2
    area = own_rows * low_cols
    shard = -(-(taps * chans) // (parts * 16)) * 16
    cores = 2 if parts % 2 == 0 else 1
    chips = parts // cores
    dma = pltpu.SemaphoreType.DMA
    vmem = pl.BlockSpec(memory_space=pltpu.VMEM)
    grad_images, grad_kernel = pl.pallas_call(
        kernel,
        out_shape=(
            jax.ShapeDtypeStruct((chans, low_rows, low_cols), BF16),
            jax.ShapeDtypeStruct((taps, all_chans, outs), F32),
        ),
        in_specs=[pl.BlockSpec(memory_space=pltpu.HBM)] * 3,
        out_specs=(vmem, vmem),
        scratch_shapes=[
            pltpu.VMEM((chans, low_rows, low_cols), BF16),
            pltpu.VMEM((outs, rows, cols), BF16),
            pltpu.VMEM((taps, all_chans, outs), BF16),
            dma((3,)),
            pltpu.VMEM((cols // 128, outs * rows, 128), F32),
            pltpu.VMEM((outs, (rows + 2) * cols), BF16),
            pltpu.VMEM((taps * outs, area), BF16),
            pltpu.VMEM((2 * cols, 3 * low_cols), BF16),
            pltpu.VMEM((all_chans, taps * outs), BF16),
            pltpu.VMEM((slabs, chans, area), BF16),
            pltpu.VMEM((slabs, chans, area), BF16),
            pltpu.VMEM((chans * low_rows, low_cols), F32),
            pltpu.VMEM((all_chans, area), BF16),
            pltpu.VMEM((slabs, chans, area), BF16),
            pltpu.VMEM((chans * low_rows, low_cols), F32),
            pltpu.VMEM((slabs, parts * shard, outs), BF16),
            pltpu.VMEM((slabs, parts, shard, outs), BF16),
            pltpu.VMEM((2, slabs, shard, outs), F32),
            pltpu.VMEM((slabs, parts * shard, outs), BF16),
            dma((2,)), dma((2,)), dma((slabs,)), dma((slabs,)), dma((slabs,)), dma((slabs,)),
            dma((slabs, parts)), dma((slabs, parts)), dma((slabs,)), dma((slabs,)),
            dma((slabs,)), dma((slabs,)), dma((slabs, chips)), dma((slabs, chips)),
            dma((slabs, chips, cores)), dma((slabs, chips, cores)),
        ],
        compiler_params=pltpu.CompilerParams(
            collective_id=0, has_side_effects=True, vmem_limit_bytes=48 * 1024 * 1024
        ),
    )(images[0], cotangent[0], weights.reshape(taps, all_chans, outs))
    return grad_images[None], grad_kernel.reshape(weights.shape)


def solution(mesh):
    placed = (P("dp", "slab", None, None), P("dp", None, "slab", None), P())
    return jax.shard_map(
        body,
        mesh=mesh,
        in_specs=placed,
        out_specs=(P("dp", "slab", None, None), P()),
        check_vma=False,
    )
```

```python
import functools

import jax
import jax.numpy as jnp
from jax import lax
from jax.experimental import pallas as pl
from jax.experimental.pallas import tpu as pltpu
from jax.sharding import PartitionSpec as P

MESH = pl.DeviceIdType.MESH
BF16 = jnp.bfloat16
F32 = jnp.float32


def each(low, high, step):
    if high - low <= 8:
        for index in range(low, high):
            step(index)
    else:
        lax.fori_loop(low, high, lambda index, carry: (step(index), carry)[1], 0)


def kernel(
    images, cotangent, weights, grad_images, grad_kernel,
    wide, rows_up, box, pairs, flat, image_send, image_all, image_wide, input_send, input_all, input_wide,
    term_send, term_all, term_sum, total,
    halo_out, halo_in, image_out, image_in, input_out, input_in, term_out, term_in, sum_out, sum_in,
    slab_out, slab_in, dp_out, dp_in, core_out, core_in,
):
    slabs, parts = lax.axis_size("slab"), lax.axis_size("dp")
    me, part = lax.axis_index("slab"), lax.axis_index("dp")
    chans, low_rows, low_cols = images.shape
    outs, rows, cols = cotangent.shape
    all_chans = chans * slabs
    taps = weights.shape[0]
    own_rows = rows // 2
    shard = term_all.shape[2]
    cores = core_out.shape[2]
    chips = parts // cores
    core = lax.rem(part, cores)

    def slab_at(distance):
        return lax.rem(me + distance + slabs, slabs)

    def part_at(distance):
        return lax.rem(part + distance + parts, parts)

    barrier = pltpu.get_barrier_semaphore()
    each(1, slabs, lambda r: pl.semaphore_signal(barrier, inc=1, device_id={"slab": slab_at(r)}, device_id_type=MESH))
    each(1, parts, lambda j: pl.semaphore_signal(barrier, inc=1, device_id={"dp": part_at(j)}, device_id_type=MESH))

    def remote(src, dst, send, recv, device):
        return pltpu.make_async_remote_copy(
            src_ref=src, dst_ref=dst, send_sem=send, recv_sem=recv, device_id=device, device_id_type=MESH
        )

    for o in range(0, outs, 16):
        for half in range(cols // 128):
            part_of = cotangent[pl.ds(o, 16), :, pl.ds(half * 128, 128)]
            wide[half, pl.ds(o * rows, 16 * rows), :] = part_of.astype(F32).reshape(16 * rows, 128)

    def turn(row):
        for half in range(cols // 128):
            rows_up[:, pl.ds((row + 1) * cols + half * 128, 128)] = wide[
                half, pl.ds(row, outs, stride=rows), :
            ].astype(BF16)

    turn(0)
    turn(rows - 1)

    image_wide[...] = images[...].astype(F32).reshape(chans * low_rows, low_cols)

    def image_block(dst, slab):
        for p in range(own_rows):
            dst[:, pl.ds(p * low_cols, low_cols)] = image_wide[
                pl.ds(slab * own_rows + p, chans, stride=low_rows), :
            ].astype(BF16)

    image_copies = [None]
    for r in range(1, slabs):
        target = slab_at(-r)
        image_block(image_send.at[r], target)
        image_copies.append(remote(image_send.at[r], image_all.at[r], image_out.at[r], image_in.at[r], {"slab": target}))

    pl.semaphore_wait(barrier, slabs - 1 + parts - 1)

    first, last = pl.ds(0, cols), pl.ds((rows + 1) * cols, cols)
    head = remote(rows_up.at[:, pl.ds(cols, cols)], rows_up.at[:, last], halo_out.at[0], halo_in.at[0], {"slab": slab_at(-1)})
    tail = remote(rows_up.at[:, pl.ds(rows * cols, cols)], rows_up.at[:, first], halo_out.at[1], halo_in.at[1], {"slab": slab_at(1)})

    @pl.when(me > 0)
    def _():
        head.start()

    @pl.when(me < slabs - 1)
    def _():
        tail.start()

    for r in range(1, slabs):
        image_copies[r].start()
    image_block(image_all.at[0], me)

    for row in range(1, rows - 1):
        turn(row)

    j = lax.broadcasted_iota(jnp.int32, (cols, low_cols), 0)
    q = lax.broadcasted_iota(jnp.int32, (cols, low_cols), 1)
    for b in range(3):
        gap = j - 2 * q + b
        hit = jnp.where((gap == 1) | (gap == 2), 1.0, 0.0).astype(BF16)
        pairs[pl.ds(0, cols), pl.ds(b * low_cols, low_cols)] = hit
        pairs[pl.ds(cols, cols), pl.ds(b * low_cols, low_cols)] = hit
    for tap in range(taps):
        flat[:, pl.ds(tap * outs, outs)] = weights[tap]

    def box_rows(places):
        around = [rows_up[:, pl.ds((2 * p - a + 2) * cols, 2 * cols)] for p, a in places]
        sums = jnp.dot(jnp.concatenate(around, axis=0), pairs[...], preferred_element_type=F32).astype(BF16)
        for n, (p, a) in enumerate(places):
            for b in range(3):
                box[pl.ds((a * 3 + b) * outs, outs), pl.ds(p * low_cols, low_cols)] = sums[
                    n * outs:(n + 1) * outs, b * low_cols:(b + 1) * low_cols
                ]

    edge = [(0, 2), (own_rows - 1, 0)]
    inner = [(p, a) for a in range(3) for p in range(own_rows) if (p, a) not in edge]
    for n in range(0, len(inner), 4):
        box_rows(inner[n:n + 4])

    @pl.when(me > 0)
    def _():
        tail.wait_recv()

    @pl.when(me == 0)
    def _():
        rows_up[:, first] = jnp.zeros((outs, cols), BF16)

    @pl.when(me < slabs - 1)
    def _():
        head.wait_recv()

    @pl.when(me == slabs - 1)
    def _():
        rows_up[:, last] = jnp.zeros((outs, cols), BF16)

    box_rows(edge)

    used = taps * chans
    padded = parts * shard

    def terms(r):
        product = lax.dot_general(
            image_all[r], box[...], (((1,), (1,)), ((), ())), preferred_element_type=F32
        ).astype(BF16)
        for tap in range(taps):
            term_send[r, pl.ds(tap * chans, chans), :] = product[:, tap * outs:(tap + 1) * outs]
        if padded > used:
            term_send[r, pl.ds(used, padded - used), :] = jnp.zeros((padded - used, outs), BF16)

    def term_copy(r, step):
        peer = part_at(step)
        return remote(
            term_send.at[r, pl.ds(pl.multiple_of(peer * shard, 16), shard)], term_all.at[r, step],
            term_out.at[r, step], term_in.at[r, step], {"dp": peer},
        )

    sum_copies = [None] * slabs

    def gather_terms(r):
        acc = term_send[r, pl.ds(pl.multiple_of(part * shard, 16), shard), :].astype(F32)
        each(1, parts, lambda step: term_copy(r, step).wait_recv())
        if parts <= 8:
            for step in range(1, parts):
                acc = acc + term_all[r, step].astype(F32)
        else:
            acc = lax.fori_loop(1, parts, lambda step, value: value + term_all[r, step].astype(F32), acc)
        if r == 0:
            term_sum[0, 0] = acc
        else:
            term_sum[1, r] = acc
            copy = remote(term_sum.at[1, r], term_sum.at[0, r], sum_out.at[r], sum_in.at[r], {"slab": slab_at(r)})
            copy.start()
            sum_copies[r] = copy

    terms(0)
    each(1, parts, lambda step: term_copy(0, step).start())

    tile = 2 * low_cols
    for n in range(own_rows * low_cols // tile):
        at = pl.ds(n * tile, tile)
        input_send[:, at] = jnp.dot(flat[...], box[:, at], preferred_element_type=F32).astype(BF16)

    input_copies = [None]
    for r in range(1, slabs):
        image_copies[r].wait_recv()
        terms(r)
        each(1, parts, lambda step: term_copy(r, step).start())
        gather_terms(r - 1)
        image_copies[r].wait_send()
        target = slab_at(-r)
        copy = remote(
            input_send.at[pl.ds(pl.multiple_of(target * chans, 16), chans)], input_all.at[me],
            input_out.at[r], input_in.at[r], {"slab": target},
        )
        copy.start()
        input_copies.append(copy)
    gather_terms(slabs - 1)
    input_all[me] = input_send[pl.ds(pl.multiple_of(me * chans, 16), chans), :]

    for r in range(1, slabs):
        sum_copies[r].wait_recv()
    mine = pl.ds(pl.multiple_of(part * shard, 16), shard)
    total[me, mine, :] = functools.reduce(lambda x, y: x + y, [term_sum[0, r] for r in range(slabs)]).astype(BF16)

    slab_copies = [None]
    for r in range(1, slabs):
        copy = remote(total.at[me, mine], total.at[me, mine], slab_out.at[r], slab_in.at[r], {"slab": slab_at(r)})
        copy.start()
        slab_copies.append(copy)

    def dp_copy(r, step):
        source = slab_at(-r)
        return remote(total.at[source, mine], total.at[source, mine], dp_out.at[r, step], dp_in.at[r, step], {"dp": part_at(step * cores)})

    def core_copy(r, step, other):
        source = slab_at(-r)
        at = pl.ds(pl.multiple_of(part_at(-step * cores) * shard, 16), shard)
        device = part - core + lax.rem(core + other, cores)
        return remote(
            total.at[source, at], total.at[source, at], core_out.at[r, step, other], core_in.at[r, step, other], {"dp": device}
        )

    def for_cores(r, step, act):
        for other in range(1, cores):
            act(core_copy(r, step, other))

    for r in range(slabs):
        if r:
            slab_copies[r].wait_recv()
        each(1, chips, lambda step: dp_copy(r, step).start())
        for_cores(r, 0, lambda copy: copy.start())

    def forward(r, step):
        dp_copy(r, step).wait_recv()
        for_cores(r, step, lambda copy: copy.start())

    for r in range(slabs):
        each(1, chips, lambda step: forward(r, step))

    for r in range(1, slabs):
        input_copies[r].wait_recv()
    for s in range(slabs):
        for p in range(own_rows):
            input_wide[pl.ds(s * own_rows + p, chans, stride=low_rows), :] = input_all[
                s, :, pl.ds(p * low_cols, low_cols)
            ].astype(F32)
    grad_images[...] = input_wide[...].astype(BF16).reshape(chans, low_rows, low_cols)

    for r in range(slabs):
        each(0, chips, lambda step: for_cores(r, step, lambda copy: copy.wait_recv()))
    for s in range(slabs):
        for tap in range(taps):
            grad_kernel[tap, pl.ds(s * chans, chans), :] = total[s, pl.ds(tap * chans, chans), :].astype(F32)

    @pl.when(me > 0)
    def _():
        head.wait_send()

    @pl.when(me < slabs - 1)
    def _():
        tail.wait_send()

    for r in range(1, slabs):
        input_copies[r].wait_send()
        sum_copies[r].wait_send()
        slab_copies[r].wait_send()
    for r in range(slabs):
        each(1, parts, lambda step: term_copy(r, step).wait_send())
        each(1, chips, lambda step: dp_copy(r, step).wait_send())
        each(0, chips, lambda step: for_cores(r, step, lambda copy: copy.wait_send()))


def body(images, cotangent, weights):
    slabs, parts = lax.axis_size("slab"), lax.axis_size("dp")
    _, chans, low_rows, low_cols = images.shape
    _, outs, rows, cols = cotangent.shape
    height, width, all_chans, _ = weights.shape
    taps = height * width
    own_rows = rows // 2
    area = own_rows * low_cols
    shard = -(-(taps * chans) // (parts * 16)) * 16
    cores = 2 if parts % 2 == 0 else 1
    chips = parts // cores
    dma = pltpu.SemaphoreType.DMA
    vmem = pl.BlockSpec(memory_space=pltpu.VMEM)
    grad_images, grad_kernel = pl.pallas_call(
        kernel,
        out_shape=(
            jax.ShapeDtypeStruct((chans, low_rows, low_cols), BF16),
            jax.ShapeDtypeStruct((taps, all_chans, outs), F32),
        ),
        in_specs=[vmem] * 3,
        out_specs=(vmem, vmem),
        scratch_shapes=[
            pltpu.VMEM((cols // 128, outs * rows, 128), F32),
            pltpu.VMEM((outs, (rows + 2) * cols), BF16),
            pltpu.VMEM((taps * outs, area), BF16),
            pltpu.VMEM((2 * cols, 3 * low_cols), BF16),
            pltpu.VMEM((all_chans, taps * outs), BF16),
            pltpu.VMEM((slabs, chans, area), BF16),
            pltpu.VMEM((slabs, chans, area), BF16),
            pltpu.VMEM((chans * low_rows, low_cols), F32),
            pltpu.VMEM((all_chans, area), BF16),
            pltpu.VMEM((slabs, chans, area), BF16),
            pltpu.VMEM((chans * low_rows, low_cols), F32),
            pltpu.VMEM((slabs, parts * shard, outs), BF16),
            pltpu.VMEM((slabs, parts, shard, outs), BF16),
            pltpu.VMEM((2, slabs, shard, outs), F32),
            pltpu.VMEM((slabs, parts * shard, outs), BF16),
            dma((2,)), dma((2,)), dma((slabs,)), dma((slabs,)), dma((slabs,)), dma((slabs,)),
            dma((slabs, parts)), dma((slabs, parts)), dma((slabs,)), dma((slabs,)),
            dma((slabs,)), dma((slabs,)), dma((slabs, chips)), dma((slabs, chips)),
            dma((slabs, chips, cores)), dma((slabs, chips, cores)),
        ],
        compiler_params=pltpu.CompilerParams(
            collective_id=0, has_side_effects=True, vmem_limit_bytes=48 * 1024 * 1024
        ),
    )(images[0], cotangent[0], weights.reshape(taps, all_chans, outs))
    return grad_images[None], grad_kernel.reshape(weights.shape)


def solution(mesh):
    placed = (P("dp", "slab", None, None), P("dp", None, "slab", None), P())
    return jax.shard_map(
        body,
        mesh=mesh,
        in_specs=placed,
        out_specs=(P("dp", "slab", None, None), P()),
        check_vma=False,
    )
```
